32 devices in a mesh: groups: 2 (over y), seq: 16 (over z, x, core).
Axes of the slice: x: 2, y: 2, z: 4, core: 2. Of those that a mesh axis runs over, the one named last changes fastest.
Arguments:
- query_in: bfloat16 [16384, 128], P(('groups', 'seq')), parts along dimension 0, may hold values from -6 to 6
- key_in: bfloat16 [16384, 128], P(('groups', 'seq')), parts along dimension 0, may hold values from -6 to 6
- value_in: bfloat16 [16384, 1024], P(('groups', 'seq')), parts along dimension 0, may hold values from -12 to 12
- conv_weight: float32 [3, 1024], replicated, may hold values from -3 to 3
- norm_gain: float32 [1024], replicated, may hold values from 0.1 to 1.9
- window_query: bfloat16 [16384, 1024], P(('groups', 'seq')), parts along dimension 0, may hold values from -6 to 6
- window_key: bfloat16 [16384, 1024], P(('groups', 'seq')), parts along dimension 0, may hold values from -6 to 6
- cotangent: bfloat16 [16384, 1024], P(('groups', 'seq')), parts along dimension 0, may hold values from -6 to 6
Outputs:
- layer_out: bfloat16 [16384, 1024], P(('groups', 'seq')), parts along dimension 0
- query_grad: bfloat16 [16384, 128], P(('groups', 'seq')), parts along dimension 0
- key_grad: bfloat16 [16384, 128], P(('groups', 'seq')), parts along dimension 0
- window_grad: bfloat16 [2, 16384, 1024], P(None, ('groups', 'seq')), parts along dimension 1
- value_grad: bfloat16 [16384, 1024], P(('groups', 'seq')), parts along dimension 0
The draws below stay inside these ranges and needn't reach their ends.
There are 2 independent parts, one for each index of `groups`. The reference program is written for one: setup_inputs(seed, part) draws one part's arguments, and reference() takes and returns one part's arrays. A program takes and returns all parts, laid end to end along the dimension named above; an argument that names none is the same for every part. Nothing has to cross between parts.
All inputs are finite; a program needn't handle non-finite values.
Results may differ from the reference program's by a relative error of at most 0.0077.
Values may be sent and summed in bfloat16 or wider, within the bound.
A program may use at most 192 MiB of HBM per device.

```python
import math
import jax
import jax.numpy as jnp
from jax import lax

TOK_DEV = 512
H = 8
DK = 16
DV = 128
WIN = 64
KC = 3
FEAT = 273
WIDTH = 1024
LENGTH = 8192


def draw_value_in(key, part):
    column_key = jax.random.fold_in(key, 11)
    fresh_key = jax.random.fold_in(key, 13)
    column_scale = jnp.exp(jax.random.uniform(column_key, (WIDTH,), jnp.float32) * math.log(10.0)) * 10.0 ** (-0.5)
    values = jnp.clip(jax.random.normal(fresh_key, (LENGTH, WIDTH), jnp.float32), -4.0, 4.0) * column_scale
    return jnp.clip(values, -12.0, 12.0).astype(jnp.bfloat16)


def window_pair(key):
    query_key = jax.random.fold_in(key, 21)
    other_key = jax.random.fold_in(key, 22)
    query_draw = jnp.clip(jax.random.normal(query_key, (LENGTH, WIDTH), jnp.float32), -6.0, 6.0)
    key_draw = jnp.clip(jax.random.normal(other_key, (LENGTH, WIDTH), jnp.float32), -6.0, 6.0)
    return (query_draw.astype(jnp.bfloat16), key_draw.astype(jnp.bfloat16))


def draw_window_query(key, part):
    return window_pair(key)[0]


def draw_window_key(key, part):
    return window_pair(key)[1]


def block_levels(own_key, shape, cuts, low, top_value):
    def one(axis_at, blocks):
        steps = jax.random.uniform(jax.random.fold_in(jax.random.fold_in(own_key, 6), axis_at), (blocks,), jnp.float32, low / len(cuts), top_value / len(cuts))
        return jnp.repeat(jnp.exp(steps), shape[axis_at] // blocks).reshape((-1,) + (1,) * (len(shape) - axis_at - 1))

    loudness = one(*cuts[0])
    for cut in cuts[1:]:
        loudness = loudness * one(*cut)
    return loudness


def bell_draw(stream_key, dims, spread, reach, pieces=(), held_as=jnp.bfloat16):
    loudness = block_levels(stream_key, dims, pieces, -0.22, 0.18) if pieces else 1.0
    array = jax.random.normal(stream_key, dims, jnp.float32) * spread * loudness
    return jnp.minimum(jnp.maximum(array, -reach), reach).astype(held_as)


def setup_inputs(seed: int = 0, part: int = 0) -> dict:
    splits = jax.random.split(jax.random.key(seed), 9)
    own_keys = jax.random.split(jax.random.fold_in(splits[8], part), 9)
    return {
        "query_in": bell_draw(own_keys[0], (LENGTH, H * DK), 1.2, 6.0, ((0, 16),)),
        "key_in": bell_draw(own_keys[1], (LENGTH, H * DK), 1.2, 6.0, ((0, 16),)),
        "value_in": draw_value_in(jax.random.fold_in(jax.random.fold_in(splits[8], part), 71), part),
        "conv_weight": bell_draw(splits[3], (KC, WIDTH), 0.6, 3.0, (), jnp.float32),
        "norm_gain": jnp.clip(1.0 + 0.18 * jax.random.normal(splits[4], (WIDTH,), jnp.float32), 0.1, 1.9),
        "window_query": draw_window_query(jax.random.fold_in(jax.random.fold_in(splits[8], part), 71), part),
        "window_key": draw_window_key(jax.random.fold_in(jax.random.fold_in(splits[8], part), 71), part),
        "cotangent": bell_draw(own_keys[7], (LENGTH, WIDTH), 1.0, 6.0, ((0, 16),)),
    }


precise = lax.Precision.HIGHEST
epsilon = 1e-05

def full_features(scaled):
    row_count = scaled.shape[0]
    outer_terms = (scaled[:, :, :, None] * scaled[:, :, None, :]).reshape(row_count, H, DK * DK) * 0.5 ** 0.5
    constant = jnp.ones((row_count, H, 1), scaled.dtype)
    return jnp.transpose(jnp.concatenate([constant, scaled, outer_terms], axis=2), (1, 2, 0))

def taylor_local(query_block, key_block):
    row_count = query_block.shape[0]
    key_scale = DK ** (-0.25)
    query_scaled = query_block.astype(jnp.float32).reshape(row_count, H, DK) * key_scale
    key_scaled = key_block.astype(jnp.float32).reshape(row_count, H, DK) * key_scale
    taylor_score = jnp.einsum('thd,shd->hts', query_scaled, key_scaled, precision=precise)
    causal = lax.broadcasted_iota(jnp.int32, (row_count, row_count), 1) <= lax.broadcasted_iota(jnp.int32, (row_count, row_count), 0)
    kernel = jnp.where(causal[None], 1.0 + taylor_score + 0.5 * taylor_score * taylor_score, 0.0)
    return (query_scaled, key_scaled, taylor_score, causal, kernel)

def window_block(query_rows, key_rows, value_rows, grad_rows, first_device):
    row_count = query_rows.shape[0]
    key_span = key_rows.shape[0]
    query_heads = query_rows.astype(jnp.float32).reshape(row_count, H, DV)
    key_heads = key_rows.astype(jnp.float32).reshape(key_span, H, DV)
    value_heads = value_rows.astype(jnp.float32).reshape(key_span, H, DV)
    grad_heads = grad_rows.astype(jnp.float32).reshape(row_count, H, DV)
    scores = jnp.einsum('thd,shd->hts', query_heads, key_heads, precision=precise) * DV ** (-0.5)
    query_index = lax.broadcasted_iota(jnp.int32, (row_count, key_span), 0)
    key_index = lax.broadcasted_iota(jnp.int32, (row_count, key_span), 1)
    allowed = (key_index > query_index) & (key_index <= query_index + WIN) & ((key_index >= WIN) | jnp.logical_not(first_device))
    masked = jnp.where(allowed[None], scores, -jnp.inf)
    row_peak = lax.optimization_barrier(jnp.max(masked, axis=2, keepdims=True))
    exponent = jnp.exp(masked - row_peak)
    attention = exponent / lax.optimization_barrier(jnp.sum(exponent, axis=2, keepdims=True))
    attention_low = lax.optimization_barrier(attention.astype(jnp.bfloat16)).astype(jnp.float32)
    window_out = jnp.einsum('hts,shd->thd', attention_low, value_heads, precision=precise)
    grad_attention = jnp.einsum('thd,shd->hts', grad_heads, value_heads, precision=precise)
    grad_scores = attention * (grad_attention - lax.optimization_barrier(jnp.sum(attention * grad_attention, axis=2, keepdims=True)))
    score_grad = lax.optimization_barrier((grad_scores * DV ** (-0.5)).astype(jnp.bfloat16)).astype(jnp.float32)
    query_win = jnp.einsum('hts,shd->thd', score_grad, key_heads, precision=precise)
    key_win = jnp.einsum('hts,thd->shd', score_grad, query_heads, precision=precise)
    value_win = jnp.einsum('hts,thd->shd', attention_low, grad_heads, precision=precise)
    return (window_out.reshape(row_count, H * DV), query_win.reshape(row_count, H * DV), key_win.reshape(key_span, H * DV), value_win.reshape(key_span, H * DV))

def window_apply(inputs):
    return window_block(inputs[0], inputs[1], inputs[2], inputs[3], inputs[4])

def reference(query_in, key_in, value_in, conv_weight, norm_gain, window_query, window_key, cotangent):
    total_rows = value_in.shape[0]
    value_width = value_in.shape[1]
    block_count = total_rows // TOK_DEV
    key_scale = DK ** (-0.25)
    padded = jnp.concatenate([jnp.zeros((KC - 1, value_width), value_in.dtype), value_in], axis=0)
    running = jnp.zeros((total_rows, value_width), jnp.float32)
    for offset in range(KC):
        begin_row = KC - 1 - offset
        running = running + conv_weight[offset] * padded[begin_row:begin_row + total_rows].astype(jnp.float32)
    conv_values = lax.optimization_barrier(running.astype(jnp.bfloat16))
    conv_float = conv_values.astype(jnp.float32).reshape(block_count, TOK_DEV, H, DV)
    query_blocks = query_in.reshape(block_count, TOK_DEV, H * DK)
    key_blocks = key_in.reshape(block_count, TOK_DEV, H * DK)

    def forward_step(state_prior, inputs):
        query_block, key_block, value_block = inputs
        query_scaled, key_scaled, taylor_score, causal, kernel = taylor_local(query_block, key_block)
        feature_query = full_features(query_scaled)
        feature_key = full_features(key_scaled)
        numerator = jnp.einsum('hts,shv->thv', kernel, value_block, precision=precise) + jnp.einsum('hft,hfv->thv', feature_query, state_prior, precision=precise)
        state_next = state_prior + jnp.einsum('hft,thv->hfv', feature_key, value_block, precision=precise)
        return (state_next, (numerator, state_prior))
    state_start = jnp.zeros((H, FEAT, DV), jnp.float32)
    final_state, (numerator, prior_blocks) = lax.scan(forward_step, state_start, (query_blocks, key_blocks, conv_float))
    gain_heads = norm_gain.reshape(H, DV)
    norm_scale = lax.rsqrt(lax.optimization_barrier(jnp.mean(numerator * numerator, axis=3, keepdims=True)) + epsilon)
    taylor_out = gain_heads * numerator * norm_scale
    query_wblocks = window_query.reshape(block_count, TOK_DEV, value_width)
    key_wblocks = window_key.reshape(block_count, TOK_DEV, value_width)
    conv_blocks = conv_values.reshape(block_count, TOK_DEV, value_width)
    grad_blocks = cotangent.reshape(block_count, TOK_DEV, value_width)
    key_tails = jnp.concatenate([jnp.zeros((1, WIN, value_width), window_key.dtype), key_wblocks[:-1, TOK_DEV - WIN:]], axis=0)
    value_tails = jnp.concatenate([jnp.zeros((1, WIN, value_width), conv_values.dtype), conv_blocks[:-1, TOK_DEV - WIN:]], axis=0)
    key_spans = jnp.concatenate([key_tails, key_wblocks], axis=1)
    value_spans = jnp.concatenate([value_tails, conv_blocks], axis=1)
    first_flags = jnp.arange(block_count) == 0
    window_out, query_win, key_win, value_win = lax.map(window_apply, (query_wblocks, key_spans, value_spans, grad_blocks, first_flags))
    layer_out = (taylor_out.reshape(block_count, TOK_DEV, value_width) + window_out).astype(jnp.bfloat16).reshape(total_rows, value_width)
    grad_taylor = cotangent.astype(jnp.float32).reshape(block_count, TOK_DEV, H, DV) * gain_heads
    numerator_grad = norm_scale * grad_taylor - numerator * norm_scale ** 3 * lax.optimization_barrier(jnp.mean(grad_taylor * numerator, axis=3, keepdims=True))

    def backward_step(adjoint_after, inputs):
        query_block, key_block, value_block, grad_block, state_prior = inputs
        query_scaled, key_scaled, taylor_score, causal, kernel = taylor_local(query_block, key_block)
        feature_query, query_pullback = jax.vjp(full_features, query_scaled)
        feature_key, key_pullback = jax.vjp(full_features, key_scaled)
        adjoint_local = jnp.einsum('hft,thv->hfv', feature_query, grad_block, precision=precise)
        kernel_grad = jnp.where(causal[None], jnp.einsum('thv,shv->hts', grad_block, value_block, precision=precise), 0.0) * (1.0 + taylor_score)
        query_inner = query_pullback(jnp.einsum('thv,hfv->hft', grad_block, state_prior, precision=precise))[0]
        key_inner = key_pullback(jnp.einsum('thv,hfv->hft', value_block, adjoint_after, precision=precise))[0]
        query_total = jnp.einsum('hts,shd->thd', kernel_grad, key_scaled, precision=precise) + query_inner
        key_total = jnp.einsum('hts,thd->shd', kernel_grad, query_scaled, precision=precise) + key_inner
        taylor_value = jnp.einsum('hts,thv->shv', kernel, grad_block, precision=precise) + jnp.einsum('hft,hfv->thv', feature_key, adjoint_after, precision=precise)
        return (adjoint_after + adjoint_local, (query_total, key_total, taylor_value))
    final_adjoint, (query_total, key_total, taylor_value) = lax.scan(backward_step, state_start, (query_blocks, key_blocks, conv_float, numerator_grad, prior_blocks), reverse=True)
    query_grad = (query_total * key_scale).reshape(total_rows, H * DK).astype(jnp.bfloat16)
    key_grad = (key_total * key_scale).reshape(total_rows, H * DK).astype(jnp.bfloat16)
    zero_rows = jnp.zeros((1, WIN, value_width), jnp.float32)
    key_next = jnp.concatenate([key_win[1:, :WIN], zero_rows], axis=0)
    value_next = jnp.concatenate([value_win[1:, :WIN], zero_rows], axis=0)
    key_final = key_win[:, WIN:].at[:, TOK_DEV - WIN:].add(key_next)
    window_value = value_win[:, WIN:].at[:, TOK_DEV - WIN:].add(value_next)
    value_total = (taylor_value.reshape(block_count, TOK_DEV, value_width) + window_value).reshape(total_rows, value_width)
    extended = jnp.concatenate([value_total, jnp.zeros((KC - 1, value_width), jnp.float32)], axis=0)
    running = jnp.zeros((total_rows, value_width), jnp.float32)
    for offset in range(KC):
        running = running + conv_weight[offset] * extended[offset:offset + total_rows]
    value_grad = running.astype(jnp.bfloat16)
    window_grad = jnp.stack([query_win.reshape(total_rows, value_width).astype(jnp.bfloat16), key_final.reshape(total_rows, value_width).astype(jnp.bfloat16)])
    return (layer_out, query_grad, key_grad, window_grad, value_grad)
```

```python
from functools import partial

import jax
import jax.numpy as jnp
import numpy as np
from jax import lax
from jax.experimental import pallas as pl
from jax.experimental.pallas import tpu as pltpu
from jax.sharding import PartitionSpec as P

H = 8
DK = 16
DV = 128
WIN = 64
KC = 3
FP = 160
RIM = WIN + 16
TAIL = 8
EPS = 1e-05
F32 = jnp.float32
BF16 = jnp.bfloat16


def feature_tables():
    e1 = np.zeros((FP, DK), np.float32)
    e2 = np.zeros((FP, DK), np.float32)
    b1 = np.zeros((FP,), np.float32)
    b2 = np.zeros((FP,), np.float32)
    w = np.zeros((FP,), np.float32)
    for i in range(DK):
        e1[i, i], b2[i], w[i] = 1, 1, 0.25
    for d in range(DK // 2 + 1):
        for i in range(DK if d < DK // 2 else DK // 2):
            f = DK + DK * d + i
            e1[f, i], e2[f, (i + d) % DK] = 1, 1
            w[f] = 1 / 32 if d == 0 else 1 / 16
    one = DK + DK * (DK // 2) + DK // 2
    b1[one], b2[one], w[one] = 1, 1, 1
    columns = np.repeat(np.stack([b1, b2, w])[:, :, None], 128, axis=2)
    rows = np.concatenate([np.stack([b1, b2, w]), np.zeros((5, FP), np.float32)])
    return np.tile(e1, (1, H)), np.tile(e2, (1, H)), columns, rows


def nn(a, b):
    return lax.dot_general(a, b, (((1,), (0,)), ((), ())), preferred_element_type=F32)


def nt(a, b):
    return lax.dot_general(a, b, (((1,), (1,)), ((), ())), preferred_element_type=F32)


def tn(a, b):
    return lax.dot_general(a, b, (((0,), (0,)), ((), ())), preferred_element_type=F32)


def split(x):
    high = x.astype(BF16)
    return high, (x - high.astype(F32)).astype(BF16)


def body(
    n, plane,
    q_ref, k_ref, v_ref, cw_ref, gain_ref, wq_ref, wk_ref, ct_ref, e1_ref, e2_ref, col_ref, row_ref,
    lo_ref, qg_ref, kg_ref, wg_ref, vg_ref,
    vrim, krim, kback_out, vback_out, kback, vback, vnext_out, vnext,
    cv, num, wo, kw, vw, ng, dq, dk,
    loc, buf_a, tot, buf_b, base, stage, buf_c,
    rim_s, rim_r, back_s, back_r, next_s, next_r, a_s, a_r, b_s, b_r, c_s, c_r,
):
    T = q_ref.shape[0]
    deep = n // plane
    own_heads = H // plane
    R = own_heads * FP
    HALF = T // 2
    me = lax.axis_index("seq")
    z = lax.div(me, plane)
    p = lax.rem(me, plane)

    def remote(src, dst, ss, rs, to):
        return pltpu.make_async_remote_copy(
            src_ref=src, dst_ref=dst, send_sem=ss, recv_sem=rs,
            device_id={"seq": to}, device_id_type=pl.DeviceIdType.MESH,
        )

    barrier = pltpu.get_barrier_semaphore()

    def greet(to):
        pl.semaphore_signal(barrier, inc=1, device_id={"seq": to}, device_id_type=pl.DeviceIdType.MESH)

    for r in range(1, plane):
        greet(z * plane + lax.rem(p + r, plane))
    for r in range(1, deep):
        greet(lax.rem(z + r, deep) * plane + p)
    pl.when(p == 0)(lambda: greet(lax.rem(me + n - 1, n)))
    pl.when(p == plane - 1)(lambda: greet(lax.rem(me + 1, n)))
    edge = jnp.where((p == 0) | (p == plane - 1), 1, 0)
    pl.semaphore_wait(barrier, plane - 1 + deep - 1 + edge)

    def rim_copies():
        return (
            remote(v_ref.at[pl.ds(T - RIM, RIM)], vrim, rim_s.at[0], rim_r.at[0], me + 1),
            remote(wk_ref.at[pl.ds(T - WIN, WIN)], krim, rim_s.at[1], rim_r.at[1], me + 1),
        )

    def back_copies():
        return (
            remote(kback_out, kback, back_s.at[0], back_r.at[0], me - 1),
            remote(vback_out, vback, back_s.at[1], back_r.at[1], me - 1),
        )

    def next_copy():
        return (remote(vnext_out, vnext, next_s.at[0], next_r.at[0], me - 1),)

    def begin(copies):
        for c in copies:
            c.start()

    def arrived(copies):
        for c in copies:
            c.wait_recv()

    def sent(copies):
        for c in copies:
            c.wait_send()

    def copies_a(i):
        out = []
        for r in range(1, plane):
            to = lax.rem(p + r, plane)
            out.append(remote(
                loc.at[i, pl.ds(pl.multiple_of(to * R, 16), R)], buf_a.at[i, r],
                a_s.at[i, r], a_r.at[i, r], z * plane + to))
        return out

    def copies_b(i):
        out = []
        for r in range(1, deep):
            to = z + r if i == 0 else z - r
            ok = to < deep if i == 0 else to >= 0
            source = z - r if i == 0 else z + r
            comes = source >= 0 if i == 0 else source < deep
            out.append((ok, comes, r, remote(
                tot.at[i], buf_b.at[i, r], b_s.at[i, r], b_r.at[i, r], to * plane + p)))
        return out

    def copies_c(i):
        out = []
        for r in range(1, plane):
            to = lax.rem(p + r, plane)
            out.append(remote(
                stage.at[i, to], buf_c.at[i, r], c_s.at[i, r], c_r.at[i, r], z * plane + to))
        return out

    def scan_a(i):
        begin(copies_a(i))
        buf_a[i, 0] = loc[i, pl.ds(pl.multiple_of(p * R, 16), R)]

    def scan_b(i):
        arrived(copies_a(i))
        total = buf_a[i, 0].astype(F32)
        for r in range(1, plane):
            total = total + buf_a[i, r].astype(F32)
        tot[i] = total.astype(BF16)
        for ok, _, _, c in copies_b(i):
            pl.when(ok)(c.start)

    def scan_c(i):
        base[...] = jnp.zeros_like(base)
        for _, comes, r, c in copies_b(i):
            @pl.when(comes)
            def _():
                c.wait_recv()
                base[...] += buf_b[i, r].astype(F32)
        running = base[...]
        order = range(plane) if i == 0 else range(plane - 1, -1, -1)
        for d in order:
            stage[i, d] = running.astype(BF16)
            running = running + buf_a[i, lax.rem(p - d + plane, plane)].astype(F32)
        begin(copies_c(i))
        buf_c[i, 0] = stage[i, p]

    def scan_end(i):
        arrived(copies_c(i))

    def scan_sent(i):
        sent(copies_a(i))
        for ok, _, _, c in copies_b(i):
            pl.when(ok)(c.wait_send)
        sent(copies_c(i))

    def prior(i, h):
        slot = lax.rem(p - lax.div(h, own_heads) + plane, plane)
        at = pl.multiple_of(lax.rem(h, own_heads) * FP, 16)
        return (buf_c[i, slot, pl.ds(at, FP), :].astype(F32) * col_ref[2]).astype(BF16)

    def cols(h):
        return pl.ds(pl.multiple_of(h * DV, DV), DV)

    def of_head(h, rows):
        return lax.div(lax.broadcasted_iota(jnp.int32, (rows, 128), 1), DK) == h

    def masked(h, x):
        return jnp.where(of_head(h, x.shape[0]), x, jnp.zeros_like(x))

    def factors(x):
        return nt(x, e1_ref[...]) + row_ref[0:1], nt(x, e2_ref[...]) + row_ref[1:2]

    def turned(x):
        return (nt(e1_ref[...], x) + col_ref[0, :, 0:1]) * (nt(e2_ref[...], x) + col_ref[1, :, 0:1])

    def heads(low, high, f):
        def step(h, carry):
            f(h)
            return carry
        lax.fori_loop(low, high, step, 0)

    pl.when(me < n - 1)(lambda: begin(rim_copies()))

    @pl.when(me == 0)
    def _():
        vrim[...] = jnp.zeros_like(vrim)
        krim[...] = jnp.zeros_like(krim)

    pl.when(me > 0)(lambda: arrived(rim_copies()))

    def conv_state(h):
        at = cols(h)
        ext = jnp.concatenate([vrim[:, at].astype(F32), v_ref[:, at].astype(F32)], axis=0)
        mixed = (
            cw_ref[0:1, at] * ext
            + cw_ref[1:2, at] * pltpu.roll(ext, 1, 0)
            + cw_ref[2:3, at] * pltpu.roll(ext, 2, 0)
        )[RIM - WIN :].astype(BF16)
        cv[:, at] = mixed
        high, low = split(turned(masked(h, k_ref[...])))
        own = mixed[WIN:]
        loc[0, pl.ds(pl.multiple_of(h * FP, 16), FP), :] = (nn(high, own) + nn(low, own)).astype(BF16)

    heads(0, H, conv_state)
    scan_a(0)

    QB = 128
    KB = QB + WIN
    not_first = me > 0

    def window(h):
        at = cols(h)
        kw[:, at] = jnp.zeros((T + WIN, DV), F32)
        vw[:, at] = jnp.zeros((T + WIN, DV), F32)
        t_at = lax.broadcasted_iota(jnp.int32, (QB, KB), 0)
        s_at = lax.broadcasted_iota(jnp.int32, (QB, KB), 1)
        band = (s_at > t_at) & (s_at <= t_at + WIN)
        for b in range(T // QB):
            rows = pl.ds(b * QB, QB)
            span = pl.ds(b * QB, KB)
            if b == 0:
                keys = jnp.concatenate([krim[:, at], wk_ref[0:QB, at]], axis=0)
                allowed = band & ((s_at >= WIN) | not_first)
            else:
                keys = wk_ref[pl.ds(b * QB - WIN, KB), at]
                allowed = band
            queries = wq_ref[rows, at]
            values = cv[span, at]
            grads = ct_ref[rows, at]
            scores = jnp.where(allowed, nt(queries, keys) * DV ** (-0.5), -jnp.inf)
            power = jnp.exp(scores - jnp.max(scores, axis=1, keepdims=True))
            attention = power / jnp.sum(power, axis=1, keepdims=True)
            low = attention.astype(BF16)
            wo[rows, at] = nn(low, values)
            grad = nt(grads, values)
            change = attention * (grad - jnp.sum(attention * grad, axis=1, keepdims=True))
            change = (change * DV ** (-0.5)).astype(BF16)
            wg_ref[0, rows, at] = nn(change, keys).astype(BF16)
            kw[span, at] += tn(change, queries)
            vw[span, at] += tn(low, grads)
        kback_out[:, at] = kw[0:WIN, at].astype(BF16)
        vback_out[:, at] = vw[0:WIN, at].astype(BF16)

    def causal(r, width):
        t_at = lax.broadcasted_iota(jnp.int32, (HALF, width), 0) + r * HALF
        return lax.broadcasted_iota(jnp.int32, (HALF, width), 1) <= t_at

    def near(h):
        at = cols(h)
        queries = masked(h, q_ref[...])
        for r in range(2):
            width = (r + 1) * HALF
            s = nt(queries[r * HALF : (r + 1) * HALF], k_ref[0:width]) * 0.25
            kernel = jnp.where(causal(r, width), 1.0 + s + 0.5 * s * s, 0.0).astype(BF16)
            num[pl.ds(r * HALF, HALF), at] = nn(kernel, cv[pl.ds(WIN, width), at])

    heads(0, 3, window)
    scan_b(0)
    heads(3, H, window)
    scan_c(0)
    pl.when(me > 0)(lambda: begin(back_copies()))
    heads(0, H, near)
    scan_end(0)

    def normed(h):
        at = cols(h)
        state = prior(0, h)
        queries = masked(h, q_ref[...])
        one, two = factors(queries)
        high, low = split(one * two)
        top = num[:, at] + nn(high, state) + nn(low, state)
        gain = gain_ref[0:1, at]
        scale = lax.rsqrt(jnp.mean(top * top, axis=1, keepdims=True) + EPS)
        lo_ref[:, at] = (gain * top * scale + wo[:, at]).astype(BF16)
        wanted = ct_ref[:, at].astype(F32) * gain
        pull = scale * wanted - top * (scale * scale * scale) * jnp.mean(wanted * top, axis=1, keepdims=True)
        pull = pull.astype(BF16)
        ng[:, at] = pull
        high, low = split(turned(queries))
        loc[1, pl.ds(pl.multiple_of(h * FP, 16), FP), :] = (nn(high, pull) + nn(low, pull)).astype(BF16)

    heads(0, H, normed)
    scan_a(1)
    dq[...] = jnp.zeros_like(dq)
    dk[...] = jnp.zeros_like(dk)

    def through(h, change, x):
        one, two = factors(x)
        out = nn((change * two).astype(BF16), e1_ref[...]) + nn((change * one).astype(BF16), e2_ref[...])
        return masked(h, out)

    def near_back(h):
        at = cols(h)
        queries = masked(h, q_ref[...])
        keys = masked(h, k_ref[...])
        for r in range(2):
            width = (r + 1) * HALF
            rows = pl.ds(r * HALF, HALF)
            mine = queries[r * HALF : (r + 1) * HALF]
            allowed = causal(r, width)
            s = nt(mine, keys[0:width]) * 0.25
            kernel = jnp.where(allowed, 1.0 + s + 0.5 * s * s, 0.0).astype(BF16)
            pull = ng[rows, at]
            change = jnp.where(allowed, nt(pull, cv[pl.ds(WIN, width), at]) * (0.25 + 0.25 * s), 0.0)
            change = change.astype(BF16)
            dq[rows, :] += nn(change, keys[0:width])
            dk[0:width, :] += tn(change, mine)
            vw[pl.ds(WIN, width), at] += tn(kernel, pull)
        dq[...] += through(h, nt(ng[:, at], prior(0, h)), queries)

    heads(0, 3, near_back)
    scan_b(1)
    heads(3, 6, near_back)
    scan_c(1)
    heads(6, H, near_back)
    qg_ref[...] = dq[...].astype(BF16)

    @pl.when(me < n - 1)
    def _():
        arrived(back_copies())
        kw[pl.ds(T, WIN), :] += kback[...].astype(F32)
        vw[pl.ds(T, WIN), :] += vback[...].astype(F32)

    wg_ref[1] = kw[pl.ds(WIN, T), :].astype(BF16)
    scan_end(1)

    def far_value(h):
        at = cols(h)
        one, two = factors(masked(h, k_ref[...]))
        high, low = split(one * two)
        state = prior(1, h)
        vw[pl.ds(WIN, T), at] += nn(high, state) + nn(low, state)
        vnext_out[:, at] = vw[pl.ds(WIN, TAIL), at]

    heads(0, H, far_value)
    pl.when(me > 0)(lambda: begin(next_copy()))

    def far_key(h):
        at = cols(h)
        dk[...] += through(h, nt(cv[pl.ds(WIN, T), at], prior(1, h)), masked(h, k_ref[...]))

    heads(0, H, far_key)
    kg_ref[...] = dk[...].astype(BF16)

    @pl.when(me == n - 1)
    def _():
        vnext[...] = jnp.zeros_like(vnext)

    pl.when(me < n - 1)(lambda: arrived(next_copy()))

    def conv_back(h):
        at = cols(h)
        ext = jnp.concatenate([vw[pl.ds(WIN, T), at], vnext[:, at]], axis=0)
        mixed = (
            cw_ref[0:1, at] * ext
            + cw_ref[1:2, at] * pltpu.roll(ext, T + TAIL - 1, 0)
            + cw_ref[2:3, at] * pltpu.roll(ext, T + TAIL - 2, 0)
        )
        vg_ref[:, at] = mixed[0:T].astype(BF16)

    heads(0, H, conv_back)

    pl.when(me < n - 1)(lambda: sent(rim_copies()))
    pl.when(me > 0)(lambda: sent(back_copies()))
    pl.when(me > 0)(lambda: sent(next_copy()))
    scan_sent(0)
    scan_sent(1)


def shards(n, query_in, key_in, value_in, conv_weight, norm_gain, window_query, window_key, cotangent):
    T, width = value_in.shape
    plane = min(H, 1 << ((n.bit_length() - 1) // 2))
    deep = n // plane
    R = H // plane * FP
    e1, e2, columns, rows = feature_tables()
    vmem = pl.BlockSpec(memory_space=pltpu.VMEM)
    dma = pltpu.SemaphoreType.DMA
    return pl.pallas_call(
        partial(body, n, plane),
        out_shape=(
            jax.ShapeDtypeStruct((T, width), BF16),
            jax.ShapeDtypeStruct((T, H * DK), BF16),
            jax.ShapeDtypeStruct((T, H * DK), BF16),
            jax.ShapeDtypeStruct((2, T, width), BF16),
            jax.ShapeDtypeStruct((T, width), BF16),
        ),
        in_specs=[vmem] * 12,
        out_specs=(vmem,) * 5,
        scratch_shapes=[
            pltpu.VMEM((RIM, width), BF16),
            pltpu.VMEM((WIN, width), BF16),
            pltpu.VMEM((WIN, width), BF16),
            pltpu.VMEM((WIN, width), BF16),
            pltpu.VMEM((WIN, width), BF16),
            pltpu.VMEM((WIN, width), BF16),
            pltpu.VMEM((TAIL, width), F32),
            pltpu.VMEM((TAIL, width), F32),
            pltpu.VMEM((T + WIN, width), BF16),
            pltpu.VMEM((T, width), F32),
            pltpu.VMEM((T, width), F32),
            pltpu.VMEM((T + WIN, width), F32),
            pltpu.VMEM((T + WIN, width), F32),
            pltpu.VMEM((T, width), BF16),
            pltpu.VMEM((T, H * DK), F32),
            pltpu.VMEM((T, H * DK), F32),
            pltpu.VMEM((2, H * FP, DV), BF16),
            pltpu.VMEM((2, plane, R, DV), BF16),
            pltpu.VMEM((2, R, DV), BF16),
            pltpu.VMEM((2, deep, R, DV), BF16),
            pltpu.VMEM((R, DV), F32),
            pltpu.VMEM((2, plane, R, DV), BF16),
            pltpu.VMEM((2, plane, R, DV), BF16),
            dma((2,)), dma((2,)), dma((2,)), dma((2,)), dma((1,)), dma((1,)),
            dma((2, plane)), dma((2, plane)), dma((2, deep)), dma((2, deep)),
            dma((2, plane)), dma((2, plane)),
        ],
        compiler_params=pltpu.CompilerParams(
            collective_id=0, has_side_effects=True, vmem_limit_bytes=56 * 1024 * 1024
        ),
    )(
        query_in, key_in, value_in, conv_weight, norm_gain.reshape(1, width), window_query, window_key,
        cotangent, jnp.asarray(e1, BF16), jnp.asarray(e2, BF16), jnp.asarray(columns), jnp.asarray(rows),
    )


def solution(mesh):
    tokens = P(("groups", "seq"), None)
    in_specs = (tokens, tokens, tokens, P(), P(), tokens, tokens, tokens)
    out_specs = (tokens, tokens, tokens, P(None, ("groups", "seq"), None), tokens)
    return jax.shard_map(
        partial(shards, mesh.shape["seq"]), mesh=mesh, in_specs=in_specs, out_specs=out_specs, check_vma=False
    )
```

```python
from functools import partial

import jax
import jax.numpy as jnp
import numpy as np
from jax import lax
from jax.experimental import pallas as pl
from jax.experimental.pallas import tpu as pltpu
from jax.sharding import PartitionSpec as P

H = 8
DK = 16
DV = 128
WIN = 64
KC = 3
FP = 160
RIM = WIN + 16
TAIL = 8
EPS = 1e-05
F32 = jnp.float32
BF16 = jnp.bfloat16


def feature_tables():
    e1 = np.zeros((FP, DK), np.float32)
    e2 = np.zeros((FP, DK), np.float32)
    b1 = np.zeros((FP,), np.float32)
    b2 = np.zeros((FP,), np.float32)
    w = np.zeros((FP,), np.float32)
    for i in range(DK):
        e1[i, i], b2[i], w[i] = 1, 1, 0.25
    for d in range(DK // 2 + 1):
        for i in range(DK if d < DK // 2 else DK // 2):
            f = DK + DK * d + i
            e1[f, i], e2[f, (i + d) % DK] = 1, 1
            w[f] = 1 / 32 if d == 0 else 1 / 16
    one = DK + DK * (DK // 2) + DK // 2
    b1[one], b2[one], w[one] = 1, 1, 1
    columns = np.repeat(np.stack([b1, b2, w])[:, :, None], 128, axis=2)
    rows = np.concatenate([np.stack([b1, b2, w]), np.zeros((5, FP), np.float32)])
    return np.tile(e1, (1, H)), np.tile(e2, (1, H)), columns, rows


def nn(a, b):
    return lax.dot_general(a, b, (((1,), (0,)), ((), ())), preferred_element_type=F32)


def nt(a, b):
    return lax.dot_general(a, b, (((1,), (1,)), ((), ())), preferred_element_type=F32)


def tn(a, b):
    return lax.dot_general(a, b, (((0,), (0,)), ((), ())), preferred_element_type=F32)


def body(
    n, plane,
    q_ref, k_ref, v_ref, cw_ref, gain_ref, wq_ref, wk_ref, ct_ref, e1_ref, e2_ref, col_ref, row_ref,
    lo_ref, qg_ref, kg_ref, wg_ref, vg_ref,
    vrim, krim, kback_out, vback_out, kback, vback, vnext_out, vnext,
    cv, num, wo, klast, vw, ng, dq, dk, pkt, pqt, pq, pk, qa, qb, ka, kb,
    loc, buf_a, tot, buf_b, base, stage, buf_c,
    rim_s, rim_r, back_s, back_r, next_s, next_r, a_s, a_r, b_s, b_r, c_s, c_r,
):
    T = q_ref.shape[0]
    deep = n // plane
    own_heads = H // plane
    R = own_heads * FP
    HALF = T // 2
    me = lax.axis_index("seq")
    z = lax.div(me, plane)
    p = lax.rem(me, plane)

    def remote(src, dst, ss, rs, to):
        return pltpu.make_async_remote_copy(
            src_ref=src, dst_ref=dst, send_sem=ss, recv_sem=rs,
            device_id={"seq": to}, device_id_type=pl.DeviceIdType.MESH,
        )

    barrier = pltpu.get_barrier_semaphore()

    def greet(to):
        pl.semaphore_signal(barrier, inc=1, device_id={"seq": to}, device_id_type=pl.DeviceIdType.MESH)

    for r in range(1, plane):
        greet(z * plane + lax.rem(p + r, plane))
    for r in range(1, deep):
        greet(lax.rem(z + r, deep) * plane + p)
    pl.when(p == 0)(lambda: greet(lax.rem(me + n - 1, n)))
    pl.when(p == plane - 1)(lambda: greet(lax.rem(me + 1, n)))
    edge = jnp.where((p == 0) | (p == plane - 1), 1, 0)
    pl.semaphore_wait(barrier, plane - 1 + deep - 1 + edge)

    def rim_copies():
        return (
            remote(v_ref.at[pl.ds(T - RIM, RIM)], vrim, rim_s.at[0], rim_r.at[0], me + 1),
            remote(wk_ref.at[pl.ds(T - WIN, WIN)], krim, rim_s.at[1], rim_r.at[1], me + 1),
        )

    def back_copies():
        return (
            remote(kback_out, kback, back_s.at[0], back_r.at[0], me - 1),
            remote(vback_out, vback, back_s.at[1], back_r.at[1], me - 1),
        )

    def next_copy():
        return (remote(vnext_out, vnext, next_s.at[0], next_r.at[0], me - 1),)

    def begin(copies):
        for c in copies:
            c.start()

    def arrived(copies):
        for c in copies:
            c.wait_recv()

    def sent(copies):
        for c in copies:
            c.wait_send()

    def copies_a(i):
        out = []
        for r in range(1, plane):
            to = lax.rem(p + r, plane)
            out.append(remote(
                loc.at[i, pl.ds(pl.multiple_of(to * R, 16), R)], buf_a.at[i, r],
                a_s.at[i, r], a_r.at[i, r], z * plane + to))
        return out

    def copies_b(i):
        out = []
        for r in range(1, deep):
            to = z + r if i == 0 else z - r
            ok = to < deep if i == 0 else to >= 0
            source = z - r if i == 0 else z + r
            comes = source >= 0 if i == 0 else source < deep
            out.append((ok, comes, r, remote(
                tot.at[i], buf_b.at[i, r], b_s.at[i, r], b_r.at[i, r], to * plane + p)))
        return out

    def copies_c(i):
        out = []
        for r in range(1, plane):
            to = lax.rem(p + r, plane)
            out.append(remote(
                stage.at[i, to], buf_c.at[i, r], c_s.at[i, r], c_r.at[i, r], z * plane + to))
        return out

    def scan_a(i):
        begin(copies_a(i))
        buf_a[i, 0] = loc[i, pl.ds(pl.multiple_of(p * R, 16), R)]

    def scan_b(i):
        arrived(copies_a(i))
        total = buf_a[i, 0].astype(F32)
        for r in range(1, plane):
            total = total + buf_a[i, r].astype(F32)
        tot[i] = total.astype(BF16)
        for ok, _, _, c in copies_b(i):
            pl.when(ok)(c.start)

    def scan_c(i):
        base[...] = jnp.zeros_like(base)
        for _, comes, r, c in copies_b(i):
            @pl.when(comes)
            def _():
                c.wait_recv()
                base[...] += buf_b[i, r].astype(F32)
        running = base[...]
        order = range(plane) if i == 0 else range(plane - 1, -1, -1)
        for d in order:
            stage[i, d] = running.astype(BF16)
            running = running + buf_a[i, lax.rem(p - d + plane, plane)].astype(F32)
        begin(copies_c(i))
        buf_c[i, 0] = stage[i, p]

    def scan_end(i):
        arrived(copies_c(i))

    def scan_sent(i):
        sent(copies_a(i))
        for ok, _, _, c in copies_b(i):
            pl.when(ok)(c.wait_send)
        sent(copies_c(i))

    def prior(i, h):
        slot = lax.rem(p - lax.div(h, own_heads) + plane, plane)
        at = pl.multiple_of(lax.rem(h, own_heads) * FP, 16)
        return (buf_c[i, slot, pl.ds(at, FP), :].astype(F32) * col_ref[2]).astype(BF16)

    def cols(h):
        return pl.ds(pl.multiple_of(h * DV, DV), DV)

    def of_head(h, rows):
        return lax.div(lax.broadcasted_iota(jnp.int32, (rows, 128), 1), DK) == h

    def masked(h, x):
        return jnp.where(of_head(h, x.shape[0]), x, jnp.zeros_like(x))

    def factors(x):
        return nt(x, e1_ref[...]) + row_ref[0:1], nt(x, e2_ref[...]) + row_ref[1:2]

    def turned(x):
        return (nt(e1_ref[...], x) + col_ref[0, :, 0:1]) * (nt(e2_ref[...], x) + col_ref[1, :, 0:1])

    def heads(low, high, f):
        def step(h, carry):
            f(h)
            return carry
        lax.fori_loop(low, high, step, 0)

    pl.when(me < n - 1)(lambda: begin(rim_copies()))

    @pl.when(me == 0)
    def _():
        vrim[...] = jnp.zeros_like(vrim)
        krim[...] = jnp.zeros_like(krim)

    def key_features(h):
        pkt[h] = turned(masked(h, k_ref[...])).astype(BF16)

    heads(0, H, key_features)
    pl.when(me > 0)(lambda: arrived(rim_copies()))

    def conv_state(h):
        at = cols(h)
        ext = jnp.concatenate([vrim[:, at].astype(F32), v_ref[:, at].astype(F32)], axis=0)
        mixed = (
            cw_ref[0:1, at] * ext
            + cw_ref[1:2, at] * pltpu.roll(ext, 1, 0)
            + cw_ref[2:3, at] * pltpu.roll(ext, 2, 0)
        )[RIM - WIN :].astype(BF16)
        cv[:, at] = mixed
        loc[0, pl.ds(pl.multiple_of(h * FP, 16), FP), :] = nn(pkt[h], mixed[WIN:]).astype(BF16)

    heads(0, H, conv_state)
    scan_a(0)

    QB = 128
    KB = QB + WIN
    not_first = me > 0

    def window(h):
        at = cols(h)
        s_at = lax.broadcasted_iota(jnp.int32, (KB, QB), 0)
        t_at = lax.broadcasted_iota(jnp.int32, (KB, QB), 1)
        band = (s_at > t_at) & (s_at <= t_at + WIN)
        blocks = range(T // QB)
        spans = [pl.ds(b * QB, KB) for b in blocks]
        rows = [pl.ds(b * QB, QB) for b in blocks]
        keys = [
            wk_ref[pl.ds(b * QB - WIN, KB), at] if b
            else jnp.concatenate([krim[:, at], wk_ref[0:QB, at]], axis=0)
            for b in blocks
        ]
        scores = [nt(keys[b], wq_ref[rows[b], at]) for b in blocks]
        grad = [nt(cv[spans[b], at], ct_ref[rows[b], at]) for b in blocks]
        low, change = [], []
        for b in blocks:
            allowed = band if b else band & ((s_at >= WIN) | not_first)
            masked_scores = jnp.where(allowed, scores[b] * DV ** (-0.5), -jnp.inf)
            power = jnp.exp(masked_scores - jnp.max(masked_scores, axis=0, keepdims=True))
            attention = power * (1.0 / jnp.sum(power, axis=0, keepdims=True))
            low.append(attention.astype(BF16))
            mean = jnp.sum(attention * grad[b], axis=0, keepdims=True)
            change.append((attention * (grad[b] - mean) * DV ** (-0.5)).astype(BF16))
        key_parts = [nn(change[b], wq_ref[rows[b], at]) for b in blocks]
        value_parts = [nn(low[b], ct_ref[rows[b], at]) for b in blocks]
        for b in blocks:
            wo[rows[b], at] = tn(low[b], cv[spans[b], at])
            wg_ref[0, rows[b], at] = tn(change[b], keys[b]).astype(BF16)
        kback_out[:, at] = key_parts[0][0:WIN].astype(BF16)
        vback_out[:, at] = value_parts[0][0:WIN].astype(BF16)
        for b in blocks:
            mid = pl.ds(b * QB, WIN)
            wg_ref[1, mid, at] = key_parts[b][WIN:QB].astype(BF16)
            vw[mid, at] = value_parts[b][WIN:QB]
            end = pl.ds(b * QB + WIN, WIN)
            if b < T // QB - 1:
                wg_ref[1, end, at] = (key_parts[b][QB:] + key_parts[b + 1][0:WIN]).astype(BF16)
                vw[end, at] = value_parts[b][QB:] + value_parts[b + 1][0:WIN]
            else:
                klast[:, at] = key_parts[b][QB:]
                vw[end, at] = value_parts[b][QB:]

    def causal(r, width):
        t_at = lax.broadcasted_iota(jnp.int32, (HALF, width), 0) + r * HALF
        return lax.broadcasted_iota(jnp.int32, (HALF, width), 1) <= t_at

    def near(h):
        at = cols(h)
        queries = masked(h, q_ref[...])
        for r in range(2):
            width = (r + 1) * HALF
            s = nt(queries[r * HALF : (r + 1) * HALF], k_ref[0:width]) * 0.25
            kernel = jnp.where(causal(r, width), 1.0 + s + 0.5 * s * s, 0.0).astype(BF16)
            num[pl.ds(r * HALF, HALF), at] = nn(kernel, cv[pl.ds(WIN, width), at])
        one, two = factors(queries)
        qa[h] = one.astype(BF16)
        qb[h] = two.astype(BF16)
        pq[h] = (one * two).astype(BF16)
        pqt[h] = turned(queries).astype(BF16)

    heads(0, 3, window)
    scan_b(0)
    heads(3, H, window)
    pl.when(me > 0)(lambda: begin(back_copies()))
    heads(0, 2, near)
    scan_c(0)
    heads(2, H, near)
    scan_end(0)

    def normed(h):
        at = cols(h)
        state = prior(0, h)
        top = num[:, at] + nn(pq[h], state)
        gain = gain_ref[0:1, at]
        scale = lax.rsqrt(jnp.mean(top * top, axis=1, keepdims=True) + EPS)
        lo_ref[:, at] = (gain * top * scale + wo[:, at]).astype(BF16)
        wanted = ct_ref[:, at].astype(F32) * gain
        pull = scale * wanted - top * (scale * scale * scale) * jnp.mean(wanted * top, axis=1, keepdims=True)
        pull = pull.astype(BF16)
        ng[:, at] = pull
        loc[1, pl.ds(pl.multiple_of(h * FP, 16), FP), :] = nn(pqt[h], pull).astype(BF16)

    heads(0, H, normed)
    scan_a(1)
    dq[...] = jnp.zeros_like(dq)
    dk[...] = jnp.zeros_like(dk)

    def through(h, change, one, two):
        out = nn((change * two.astype(F32)).astype(BF16), e1_ref[...])
        out = out + nn((change * one.astype(F32)).astype(BF16), e2_ref[...])
        return masked(h, out)

    def near_back(h):
        at = cols(h)
        queries = masked(h, q_ref[...])
        keys = masked(h, k_ref[...])
        for r in range(2):
            width = (r + 1) * HALF
            rows = pl.ds(r * HALF, HALF)
            mine = queries[r * HALF : (r + 1) * HALF]
            allowed = causal(r, width)
            s = nt(mine, keys[0:width]) * 0.25
            kernel = jnp.where(allowed, 1.0 + s + 0.5 * s * s, 0.0).astype(BF16)
            pull = ng[rows, at]
            change = jnp.where(allowed, nt(pull, cv[pl.ds(WIN, width), at]) * (0.25 + 0.25 * s), 0.0)
            change = change.astype(BF16)
            dq[rows, :] += nn(change, keys[0:width])
            dk[0:width, :] += tn(change, mine)
            vw[pl.ds(0, width), at] += tn(kernel, pull)
        dq[...] += through(h, nt(ng[:, at], prior(0, h)), qa[h], qb[h])

    def key_factors(h):
        one, two = factors(masked(h, k_ref[...]))
        ka[h] = one.astype(BF16)
        kb[h] = two.astype(BF16)
        pk[h] = (one * two).astype(BF16)

    heads(0, 3, near_back)
    scan_b(1)
    heads(3, H, near_back)
    scan_c(1)
    heads(0, H, key_factors)
    qg_ref[...] = dq[...].astype(BF16)

    @pl.when(me < n - 1)
    def _():
        arrived(back_copies())
        klast[...] += kback[...].astype(F32)
        vw[pl.ds(T - WIN, WIN), :] += vback[...].astype(F32)

    wg_ref[1, pl.ds(T - WIN, WIN), :] = klast[...].astype(BF16)
    scan_end(1)

    def far_value(h):
        at = cols(h)
        vw[:, at] += nn(pk[h], prior(1, h))
        vnext_out[:, at] = vw[0:TAIL, at]

    heads(0, H, far_value)
    pl.when(me > 0)(lambda: begin(next_copy()))

    def far_key(h):
        at = cols(h)
        dk[...] += through(h, nt(cv[pl.ds(WIN, T), at], prior(1, h)), ka[h], kb[h])

    heads(0, H, far_key)
    kg_ref[...] = dk[...].astype(BF16)

    @pl.when(me == n - 1)
    def _():
        vnext[...] = jnp.zeros_like(vnext)

    pl.when(me < n - 1)(lambda: arrived(next_copy()))

    def conv_back(h):
        at = cols(h)
        ext = jnp.concatenate([vw[:, at], vnext[:, at]], axis=0)
        mixed = (
            cw_ref[0:1, at] * ext
            + cw_ref[1:2, at] * pltpu.roll(ext, T + TAIL - 1, 0)
            + cw_ref[2:3, at] * pltpu.roll(ext, T + TAIL - 2, 0)
        )
        vg_ref[:, at] = mixed[0:T].astype(BF16)

    heads(0, H, conv_back)

    pl.when(me < n - 1)(lambda: sent(rim_copies()))
    pl.when(me > 0)(lambda: sent(back_copies()))
    pl.when(me > 0)(lambda: sent(next_copy()))
    scan_sent(0)
    scan_sent(1)


def copies(*refs):
    count = len(refs) // 2
    for i in range(count):
        refs[count + i][...] = refs[i][...]


def handed_on(arrays):
    steps = 4

    def block(a):
        lead = a.ndim - 2
        return pl.BlockSpec(
            (*a.shape[:lead], a.shape[lead] // steps, a.shape[-1]), lambda i: (0,) * lead + (i, 0)
        )

    return pl.pallas_call(
        copies,
        grid=(steps,),
        out_shape=tuple(jax.ShapeDtypeStruct(a.shape, a.dtype) for a in arrays),
        in_specs=[block(a) for a in arrays],
        out_specs=tuple(block(a) for a in arrays),
    )(*arrays)


def shards(n, query_in, key_in, value_in, conv_weight, norm_gain, window_query, window_key, cotangent):
    T, width = value_in.shape
    plane = min(H, 1 << ((n.bit_length() - 1) // 2))
    deep = n // plane
    R = H // plane * FP
    e1, e2, columns, rows = feature_tables()
    vmem = pl.BlockSpec(memory_space=pltpu.VMEM)
    dma = pltpu.SemaphoreType.DMA
    outs = pl.pallas_call(
        partial(body, n, plane),
        out_shape=(
            jax.ShapeDtypeStruct((T, width), BF16),
            jax.ShapeDtypeStruct((T, H * DK), BF16),
            jax.ShapeDtypeStruct((T, H * DK), BF16),
            jax.ShapeDtypeStruct((2, T, width), BF16),
            jax.ShapeDtypeStruct((T, width), BF16),
        ),
        in_specs=[vmem] * 12,
        out_specs=(vmem,) * 5,
        scratch_shapes=[
            pltpu.VMEM((RIM, width), BF16),
            pltpu.VMEM((WIN, width), BF16),
            pltpu.VMEM((WIN, width), BF16),
            pltpu.VMEM((WIN, width), BF16),
            pltpu.VMEM((WIN, width), BF16),
            pltpu.VMEM((WIN, width), BF16),
            pltpu.VMEM((TAIL, width), F32),
            pltpu.VMEM((TAIL, width), F32),
            pltpu.VMEM((T + WIN, width), BF16),
            pltpu.VMEM((T, width), F32),
            pltpu.VMEM((T, width), F32),
            pltpu.VMEM((WIN, width), F32),
            pltpu.VMEM((T, width), F32),
            pltpu.VMEM((T, width), BF16),
            pltpu.VMEM((T, H * DK), F32),
            pltpu.VMEM((T, H * DK), F32),
            pltpu.VMEM((H, FP, T), BF16),
            pltpu.VMEM((H, FP, T), BF16),
            *[pltpu.VMEM((H, T, FP), BF16)] * 6,
            pltpu.VMEM((2, H * FP, DV), BF16),
            pltpu.VMEM((2, plane, R, DV), BF16),
            pltpu.VMEM((2, R, DV), BF16),
            pltpu.VMEM((2, deep, R, DV), BF16),
            pltpu.VMEM((R, DV), F32),
            pltpu.VMEM((2, plane, R, DV), BF16),
            pltpu.VMEM((2, plane, R, DV), BF16),
            dma((2,)), dma((2,)), dma((2,)), dma((2,)), dma((1,)), dma((1,)),
            dma((2, plane)), dma((2, plane)), dma((2, deep)), dma((2, deep)),
            dma((2, plane)), dma((2, plane)),
        ],
        compiler_params=pltpu.CompilerParams(
            collective_id=0, has_side_effects=True, vmem_limit_bytes=56 * 1024 * 1024
        ),
    )(
        query_in, key_in, value_in, conv_weight, norm_gain.reshape(1, width), window_query, window_key,
        cotangent, jnp.asarray(e1, BF16), jnp.asarray(e2, BF16), jnp.asarray(columns), jnp.asarray(rows),
    )
    return handed_on(outs)


def solution(mesh):
    tokens = P(("groups", "seq"), None)
    in_specs = (tokens, tokens, tokens, P(), P(), tokens, tokens, tokens)
    out_specs = (tokens, tokens, tokens, P(None, ("groups", "seq"), None), tokens)
    return jax.shard_map(
        partial(shards, mesh.shape["seq"]), mesh=mesh, in_specs=in_specs, out_specs=out_specs, check_vma=False
    )
```

```python
from functools import partial

import jax
import jax.numpy as jnp
import numpy as np
from jax import lax
from jax.experimental import pallas as pl
from jax.experimental.pallas import tpu as pltpu
from jax.sharding import PartitionSpec as P

H = 8
DK = 16
DV = 128
WIN = 64
KC = 3
FP = 160
RIM = WIN + 16
TAIL = 8
EPS = 1e-05
F32 = jnp.float32
BF16 = jnp.bfloat16


def feature_tables():
    e1 = np.zeros((FP, DK), np.float32)
    e2 = np.zeros((FP, DK), np.float32)
    b1 = np.zeros((FP,), np.float32)
    b2 = np.zeros((FP,), np.float32)
    w = np.zeros((FP,), np.float32)
    for i in range(DK):
        e1[i, i], b2[i], w[i] = 1, 1, 0.25
    for d in range(DK // 2 + 1):
        for i in range(DK if d < DK // 2 else DK // 2):
            f = DK + DK * d + i
            e1[f, i], e2[f, (i + d) % DK] = 1, 1
            w[f] = 1 / 32 if d == 0 else 1 / 16
    one = DK + DK * (DK // 2) + DK // 2
    b1[one], b2[one], w[one] = 1, 1, 1
    columns = np.repeat(np.stack([b1, b2, w])[:, :, None], 128, axis=2)
    rows = np.concatenate([np.stack([b1, b2, w]), np.zeros((5, FP), np.float32)])
    return np.tile(e1, (1, H)), np.tile(e2, (1, H)), columns, rows


def nn(a, b):
    return lax.dot_general(a, b, (((1,), (0,)), ((), ())), preferred_element_type=F32)


def nt(a, b):
    return lax.dot_general(a, b, (((1,), (1,)), ((), ())), preferred_element_type=F32)


def tn(a, b):
    return lax.dot_general(a, b, (((0,), (0,)), ((), ())), preferred_element_type=F32)


def body(
    n, plane,
    q_ref, k_ref, v_ref, cw_ref, gain_ref, wq_hbm, wk_ref, ct_hbm, e1_ref, e2_ref, col_ref, row_ref,
    lo_hbm, qg_ref, kg_ref, wg_hbm, vg_ref,
    wq_ref, ct_ref, lo_ref, wg_ref, local,
    vrim, krim, kback_out, vback_out, kback, vback, vnext_out, vnext,
    cv, num, wo, klast, vw, ng, dq, dk, pkt, pqt, pq, pk, qa, qb, ka, kb,
    loc, buf_a, tot, buf_b, base, stage, buf_c,
    rim_s, rim_r, back_s, back_r, next_s, next_r, a_s, a_r, b_s, b_r, c_s, c_r,
):
    T = q_ref.shape[0]
    deep = n // plane
    own_heads = H // plane
    R = own_heads * FP
    HALF = T // 2
    me = lax.axis_index("seq")
    z = lax.div(me, plane)
    p = lax.rem(me, plane)

    def remote(src, dst, ss, rs, to):
        return pltpu.make_async_remote_copy(
            src_ref=src, dst_ref=dst, send_sem=ss, recv_sem=rs,
            device_id={"seq": to}, device_id_type=pl.DeviceIdType.MESH,
        )

    wq_in = pltpu.make_async_copy(wq_hbm, wq_ref, local.at[0])
    ct_in = pltpu.make_async_copy(ct_hbm, ct_ref, local.at[1])
    lo_out = pltpu.make_async_copy(lo_ref, lo_hbm, local.at[2])
    wg_out = pltpu.make_async_copy(wg_ref, wg_hbm, local.at[3])
    wq_in.start()
    ct_in.start()

    barrier = pltpu.get_barrier_semaphore()

    def greet(to):
        pl.semaphore_signal(barrier, inc=1, device_id={"seq": to}, device_id_type=pl.DeviceIdType.MESH)

    for r in range(1, plane):
        greet(z * plane + lax.rem(p + r, plane))
    for r in range(1, deep):
        greet(lax.rem(z + r, deep) * plane + p)
    pl.when(p == 0)(lambda: greet(lax.rem(me + n - 1, n)))
    pl.when(p == plane - 1)(lambda: greet(lax.rem(me + 1, n)))
    edge = jnp.where((p == 0) | (p == plane - 1), 1, 0)
    pl.semaphore_wait(barrier, plane - 1 + deep - 1 + edge)

    def rim_copies():
        return (
            remote(v_ref.at[pl.ds(T - RIM, RIM)], vrim, rim_s.at[0], rim_r.at[0], me + 1),
            remote(wk_ref.at[pl.ds(T - WIN, WIN)], krim, rim_s.at[1], rim_r.at[1], me + 1),
        )

    def back_copies():
        return (
            remote(kback_out, kback, back_s.at[0], back_r.at[0], me - 1),
            remote(vback_out, vback, back_s.at[1], back_r.at[1], me - 1),
        )

    def next_copy():
        return (remote(vnext_out, vnext, next_s.at[0], next_r.at[0], me - 1),)

    def begin(copies):
        for c in copies:
            c.start()

    def arrived(copies):
        for c in copies:
            c.wait_recv()

    def sent(copies):
        for c in copies:
            c.wait_send()

    def copies_a(i):
        out = []
        for r in range(1, plane):
            to = lax.rem(p + r, plane)
            out.append(remote(
                loc.at[i, pl.ds(pl.multiple_of(to * R, 16), R)], buf_a.at[i, r],
                a_s.at[i, r], a_r.at[i, r], z * plane + to))
        return out

    def copies_b(i):
        out = []
        for r in range(1, deep):
            to = z + r if i == 0 else z - r
            ok = to < deep if i == 0 else to >= 0
            source = z - r if i == 0 else z + r
            comes = source >= 0 if i == 0 else source < deep
            out.append((ok, comes, r, remote(
                tot.at[i], buf_b.at[i, r], b_s.at[i, r], b_r.at[i, r], to * plane + p)))
        return out

    def copies_c(i):
        out = []
        for r in range(1, plane):
            to = lax.rem(p + r, plane)
            out.append(remote(
                stage.at[i, to], buf_c.at[i, r], c_s.at[i, r], c_r.at[i, r], z * plane + to))
        return out

    def scan_a(i):
        begin(copies_a(i))
        buf_a[i, 0] = loc[i, pl.ds(pl.multiple_of(p * R, 16), R)]

    def scan_b(i):
        arrived(copies_a(i))
        total = buf_a[i, 0].astype(F32)
        for r in range(1, plane):
            total = total + buf_a[i, r].astype(F32)
        tot[i] = total.astype(BF16)
        for ok, _, _, c in copies_b(i):
            pl.when(ok)(c.start)

    def scan_c(i):
        base[...] = jnp.zeros_like(base)
        for _, comes, r, c in copies_b(i):
            @pl.when(comes)
            def _():
                c.wait_recv()
                base[...] += buf_b[i, r].astype(F32)
        running = base[...]
        order = range(plane) if i == 0 else range(plane - 1, -1, -1)
        for d in order:
            stage[i, d] = running.astype(BF16)
            running = running + buf_a[i, lax.rem(p - d + plane, plane)].astype(F32)
        begin(copies_c(i))
        buf_c[i, 0] = stage[i, p]

    def scan_end(i):
        arrived(copies_c(i))

    def scan_sent(i):
        sent(copies_a(i))
        for ok, _, _, c in copies_b(i):
            pl.when(ok)(c.wait_send)
        sent(copies_c(i))

    def prior(i, h):
        slot = lax.rem(p - lax.div(h, own_heads) + plane, plane)
        at = pl.multiple_of(lax.rem(h, own_heads) * FP, 16)
        return (buf_c[i, slot, pl.ds(at, FP), :].astype(F32) * col_ref[2]).astype(BF16)

    def cols(h):
        return pl.ds(pl.multiple_of(h * DV, DV), DV)

    def of_head(h, rows):
        return lax.div(lax.broadcasted_iota(jnp.int32, (rows, 128), 1), DK) == h

    def masked(h, x):
        return jnp.where(of_head(h, x.shape[0]), x, jnp.zeros_like(x))

    def factors(x):
        return nt(x, e1_ref[...]) + row_ref[0:1], nt(x, e2_ref[...]) + row_ref[1:2]

    def turned(x):
        return (nt(e1_ref[...], x) + col_ref[0, :, 0:1]) * (nt(e2_ref[...], x) + col_ref[1, :, 0:1])

    def heads(low, high, f):
        def step(h, carry):
            f(h)
            return carry
        lax.fori_loop(low, high, step, 0)

    pl.when(me < n - 1)(lambda: begin(rim_copies()))

    @pl.when(me == 0)
    def _():
        vrim[...] = jnp.zeros_like(vrim)
        krim[...] = jnp.zeros_like(krim)

    def key_features(h):
        pkt[h] = turned(masked(h, k_ref[...])).astype(BF16)

    heads(0, H, key_features)
    pl.when(me > 0)(lambda: arrived(rim_copies()))

    def conv_state(h):
        at = cols(h)
        ext = jnp.concatenate([vrim[:, at].astype(F32), v_ref[:, at].astype(F32)], axis=0)
        mixed = (
            cw_ref[0:1, at] * ext
            + cw_ref[1:2, at] * pltpu.roll(ext, 1, 0)
            + cw_ref[2:3, at] * pltpu.roll(ext, 2, 0)
        )[RIM - WIN :].astype(BF16)
        cv[:, at] = mixed
        loc[0, pl.ds(pl.multiple_of(h * FP, 16), FP), :] = nn(pkt[h], mixed[WIN:]).astype(BF16)

    heads(0, H, conv_state)
    scan_a(0)

    QB = 128
    KB = QB + WIN
    not_first = me > 0

    def window(h):
        at = cols(h)
        s_at = lax.broadcasted_iota(jnp.int32, (KB, QB), 0)
        t_at = lax.broadcasted_iota(jnp.int32, (KB, QB), 1)
        band = (s_at > t_at) & (s_at <= t_at + WIN)
        blocks = range(T // QB)
        spans = [pl.ds(b * QB, KB) for b in blocks]
        rows = [pl.ds(b * QB, QB) for b in blocks]
        keys = [
            wk_ref[pl.ds(b * QB - WIN, KB), at] if b
            else jnp.concatenate([krim[:, at], wk_ref[0:QB, at]], axis=0)
            for b in blocks
        ]
        scores = [nt(keys[b], wq_ref[rows[b], at]) for b in blocks]
        grad = [nt(cv[spans[b], at], ct_ref[rows[b], at]) for b in blocks]
        low, change = [], []
        for b in blocks:
            allowed = band if b else band & ((s_at >= WIN) | not_first)
            masked_scores = jnp.where(allowed, scores[b] * DV ** (-0.5), -jnp.inf)
            power = jnp.exp(masked_scores - jnp.max(masked_scores, axis=0, keepdims=True))
            attention = power * (1.0 / jnp.sum(power, axis=0, keepdims=True))
            low.append(attention.astype(BF16))
            mean = jnp.sum(attention * grad[b], axis=0, keepdims=True)
            change.append((attention * (grad[b] - mean) * DV ** (-0.5)).astype(BF16))
        key_parts = [nn(change[b], wq_ref[rows[b], at]) for b in blocks]
        value_parts = [nn(low[b], ct_ref[rows[b], at]) for b in blocks]
        for b in blocks:
            wo[rows[b], at] = tn(low[b], cv[spans[b], at])
            wg_ref[0, rows[b], at] = tn(change[b], keys[b]).astype(BF16)
        kback_out[:, at] = key_parts[0][0:WIN].astype(BF16)
        vback_out[:, at] = value_parts[0][0:WIN].astype(BF16)
        for b in blocks:
            mid = pl.ds(b * QB, WIN)
            wg_ref[1, mid, at] = key_parts[b][WIN:QB].astype(BF16)
            vw[mid, at] = value_parts[b][WIN:QB]
            end = pl.ds(b * QB + WIN, WIN)
            if b < T // QB - 1:
                wg_ref[1, end, at] = (key_parts[b][QB:] + key_parts[b + 1][0:WIN]).astype(BF16)
                vw[end, at] = value_parts[b][QB:] + value_parts[b + 1][0:WIN]
            else:
                klast[:, at] = key_parts[b][QB:]
                vw[end, at] = value_parts[b][QB:]

    def causal(r, width):
        t_at = lax.broadcasted_iota(jnp.int32, (HALF, width), 0) + r * HALF
        return lax.broadcasted_iota(jnp.int32, (HALF, width), 1) <= t_at

    def near(h):
        at = cols(h)
        queries = masked(h, q_ref[...])
        for r in range(2):
            width = (r + 1) * HALF
            s = nt(queries[r * HALF : (r + 1) * HALF], k_ref[0:width]) * 0.25
            kernel = jnp.where(causal(r, width), 1.0 + s + 0.5 * s * s, 0.0).astype(BF16)
            num[pl.ds(r * HALF, HALF), at] = nn(kernel, cv[pl.ds(WIN, width), at])
        one, two = factors(queries)
        qa[h] = one.astype(BF16)
        qb[h] = two.astype(BF16)
        pq[h] = (one * two).astype(BF16)
        pqt[h] = turned(queries).astype(BF16)

    wq_in.wait()
    ct_in.wait()
    heads(0, 3, window)
    scan_b(0)
    heads(3, H, window)
    pl.when(me > 0)(lambda: begin(back_copies()))
    heads(0, 2, near)
    scan_c(0)
    heads(2, H, near)
    scan_end(0)

    def normed(h):
        at = cols(h)
        state = prior(0, h)
        top = num[:, at] + nn(pq[h], state)
        gain = gain_ref[0:1, at]
        scale = lax.rsqrt(jnp.mean(top * top, axis=1, keepdims=True) + EPS)
        lo_ref[:, at] = (gain * top * scale + wo[:, at]).astype(BF16)
        wanted = ct_ref[:, at].astype(F32) * gain
        pull = scale * wanted - top * (scale * scale * scale) * jnp.mean(wanted * top, axis=1, keepdims=True)
        pull = pull.astype(BF16)
        ng[:, at] = pull
        loc[1, pl.ds(pl.multiple_of(h * FP, 16), FP), :] = nn(pqt[h], pull).astype(BF16)

    heads(0, H, normed)
    scan_a(1)
    lo_out.start()
    dq[...] = jnp.zeros_like(dq)
    dk[...] = jnp.zeros_like(dk)

    def through(h, change, one, two):
        out = nn((change * two.astype(F32)).astype(BF16), e1_ref[...])
        out = out + nn((change * one.astype(F32)).astype(BF16), e2_ref[...])
        return masked(h, out)

    def near_back(h):
        at = cols(h)
        queries = masked(h, q_ref[...])
        keys = masked(h, k_ref[...])
        for r in range(2):
            width = (r + 1) * HALF
            rows = pl.ds(r * HALF, HALF)
            mine = queries[r * HALF : (r + 1) * HALF]
            allowed = causal(r, width)
            s = nt(mine, keys[0:width]) * 0.25
            kernel = jnp.where(allowed, 1.0 + s + 0.5 * s * s, 0.0).astype(BF16)
            pull = ng[rows, at]
            change = jnp.where(allowed, nt(pull, cv[pl.ds(WIN, width), at]) * (0.25 + 0.25 * s), 0.0)
            change = change.astype(BF16)
            dq[rows, :] += nn(change, keys[0:width])
            dk[0:width, :] += tn(change, mine)
            vw[pl.ds(0, width), at] += tn(kernel, pull)
        dq[...] += through(h, nt(ng[:, at], prior(0, h)), qa[h], qb[h])

    def key_factors(h):
        one, two = factors(masked(h, k_ref[...]))
        ka[h] = one.astype(BF16)
        kb[h] = two.astype(BF16)
        pk[h] = (one * two).astype(BF16)

    heads(0, 3, near_back)
    scan_b(1)
    heads(3, H, near_back)
    scan_c(1)
    heads(0, H, key_factors)
    qg_ref[...] = dq[...].astype(BF16)

    @pl.when(me < n - 1)
    def _():
        arrived(back_copies())
        klast[...] += kback[...].astype(F32)
        vw[pl.ds(T - WIN, WIN), :] += vback[...].astype(F32)

    wg_ref[1, pl.ds(T - WIN, WIN), :] = klast[...].astype(BF16)
    wg_out.start()
    scan_end(1)

    def far_value(h):
        at = cols(h)
        vw[:, at] += nn(pk[h], prior(1, h))
        vnext_out[:, at] = vw[0:TAIL, at]

    heads(0, H, far_value)
    pl.when(me > 0)(lambda: begin(next_copy()))

    def far_key(h):
        at = cols(h)
        dk[...] += through(h, nt(cv[pl.ds(WIN, T), at], prior(1, h)), ka[h], kb[h])

    heads(0, H, far_key)
    kg_ref[...] = dk[...].astype(BF16)

    @pl.when(me == n - 1)
    def _():
        vnext[...] = jnp.zeros_like(vnext)

    pl.when(me < n - 1)(lambda: arrived(next_copy()))

    def conv_back(h):
        at = cols(h)
        ext = jnp.concatenate([vw[:, at], vnext[:, at]], axis=0)
        mixed = (
            cw_ref[0:1, at] * ext
            + cw_ref[1:2, at] * pltpu.roll(ext, T + TAIL - 1, 0)
            + cw_ref[2:3, at] * pltpu.roll(ext, T + TAIL - 2, 0)
        )
        vg_ref[:, at] = mixed[0:T].astype(BF16)

    heads(0, H, conv_back)

    pl.when(me < n - 1)(lambda: sent(rim_copies()))
    pl.when(me > 0)(lambda: sent(back_copies()))
    pl.when(me > 0)(lambda: sent(next_copy()))
    scan_sent(0)
    scan_sent(1)
    lo_out.wait()
    wg_out.wait()


def copies(*refs):
    count = len(refs) // 2
    for i in range(count):
        refs[count + i][...] = refs[i][...]


def handed_on(arrays):
    steps = 4

    def block(a):
        lead = a.ndim - 2
        return pl.BlockSpec(
            (*a.shape[:lead], a.shape[lead] // steps, a.shape[-1]), lambda i: (0,) * lead + (i, 0)
        )

    return pl.pallas_call(
        copies,
        grid=(steps,),
        out_shape=tuple(jax.ShapeDtypeStruct(a.shape, a.dtype) for a in arrays),
        in_specs=[block(a) for a in arrays],
        out_specs=tuple(block(a) for a in arrays),
    )(*arrays)


def shards(n, query_in, key_in, value_in, conv_weight, norm_gain, window_query, window_key, cotangent):
    T, width = value_in.shape
    plane = min(H, 1 << ((n.bit_length() - 1) // 2))
    deep = n // plane
    R = H // plane * FP
    e1, e2, columns, rows = feature_tables()
    vmem = pl.BlockSpec(memory_space=pltpu.VMEM)
    hbm = pl.BlockSpec(memory_space=pl.ANY)
    dma = pltpu.SemaphoreType.DMA
    outs = pl.pallas_call(
        partial(body, n, plane),
        out_shape=(
            jax.ShapeDtypeStruct((T, width), BF16),
            jax.ShapeDtypeStruct((T, H * DK), BF16),
            jax.ShapeDtypeStruct((T, H * DK), BF16),
            jax.ShapeDtypeStruct((2, T, width), BF16),
            jax.ShapeDtypeStruct((T, width), BF16),
        ),
        in_specs=[vmem] * 5 + [hbm, vmem, hbm] + [vmem] * 4,
        out_specs=(hbm, vmem, vmem, hbm, vmem),
        scratch_shapes=[
            pltpu.VMEM((T, width), BF16),
            pltpu.VMEM((T, width), BF16),
            pltpu.VMEM((T, width), BF16),
            pltpu.VMEM((2, T, width), BF16),
            dma((4,)),
            pltpu.VMEM((RIM, width), BF16),
            pltpu.VMEM((WIN, width), BF16),
            pltpu.VMEM((WIN, width), BF16),
            pltpu.VMEM((WIN, width), BF16),
            pltpu.VMEM((WIN, width), BF16),
            pltpu.VMEM((WIN, width), BF16),
            pltpu.VMEM((TAIL, width), F32),
            pltpu.VMEM((TAIL, width), F32),
            pltpu.VMEM((T + WIN, width), BF16),
            pltpu.VMEM((T, width), F32),
            pltpu.VMEM((T, width), F32),
            pltpu.VMEM((WIN, width), F32),
            pltpu.VMEM((T, width), F32),
            pltpu.VMEM((T, width), BF16),
            pltpu.VMEM((T, H * DK), F32),
            pltpu.VMEM((T, H * DK), F32),
            pltpu.VMEM((H, FP, T), BF16),
            pltpu.VMEM((H, FP, T), BF16),
            *[pltpu.VMEM((H, T, FP), BF16)] * 6,
            pltpu.VMEM((2, H * FP, DV), BF16),
            pltpu.VMEM((2, plane, R, DV), BF16),
            pltpu.VMEM((2, R, DV), BF16),
            pltpu.VMEM((2, deep, R, DV), BF16),
            pltpu.VMEM((R, DV), F32),
            pltpu.VMEM((2, plane, R, DV), BF16),
            pltpu.VMEM((2, plane, R, DV), BF16),
            dma((2,)), dma((2,)), dma((2,)), dma((2,)), dma((1,)), dma((1,)),
            dma((2, plane)), dma((2, plane)), dma((2, deep)), dma((2, deep)),
            dma((2, plane)), dma((2, plane)),
        ],
        compiler_params=pltpu.CompilerParams(
            collective_id=0, has_side_effects=True, vmem_limit_bytes=56 * 1024 * 1024
        ),
    )(
        query_in, key_in, value_in, conv_weight, norm_gain.reshape(1, width), window_query, window_key,
        cotangent, jnp.asarray(e1, BF16), jnp.asarray(e2, BF16), jnp.asarray(columns), jnp.asarray(rows),
    )
    return handed_on(outs)


def solution(mesh):
    tokens = P(("groups", "seq"), None)
    in_specs = (tokens, tokens, tokens, P(), P(), tokens, tokens, tokens)
    out_specs = (tokens, tokens, tokens, P(None, ("groups", "seq"), None), tokens)
    return jax.shard_map(
        partial(shards, mesh.shape["seq"]), mesh=mesh, in_specs=in_specs, out_specs=out_specs, check_vma=False
    )
```
